32 devices in a mesh: row: 4 (over y, x), col: 8 (over z, core).
Axes of the slice: x: 2, y: 2, z: 4, core: 2. Of those that a mesh axis runs over, the one named last changes fastest.
Arguments:
- front: float32 [16, 1024, 8, 2048], P(None, 'row', None, 'col'), may hold values from -6 to 6
- children: float32 [8, 4096, 4096], P('row', None, 'col'), may hold values from -6 to 6
- child_rows: int32 [8, 16], replicated, may hold values from 0 to 63, as said below
- owner_slots: int32 [8], replicated, may hold values from 0 to 1, as said below
- inverses: float32 [3, 256, 256], replicated, may hold values from -0.0390625 to 0.0390625
- pattern: int32 [64, 64], replicated, may hold values 0 or 1
Outputs:
- factored: float32 [16, 1024, 8, 2048], P(None, 'row', None, 'col')
The draws below stay inside these ranges and needn't reach their ends.
Inputs may be any that keep to these rules, and one draw needn't show every extreme that they name: `child_rows`: the 16 entries of one slot are distinct. For each slot g there is an offset o_g such that entry k taken mod 8 equals (k // (16 / 8) + o_g) mod 8, and every offset 0 to 8 - 1 belongs to exactly 8 / 8 slots. Hence each residue mod 4 appears exactly 16 / 4 times in each slot. `owner_slots`: slots g = o * 2 + s belong to owner o; an owner's live slots come first, slot 0 of every owner is live, at least one owner has all 2 slots live and at least one other owner has fewer.
All inputs are finite; a program needn't handle non-finite values.
Results may differ from the reference program's by a relative error of at most 0.00014.
Values sent between devices are 32-bit elements; how exact they have to be, the bound alone decides.
A program may use at most 320 MiB of HBM per device.

```python
import jax
import jax.numpy as jnp
from jax import lax

F = 16384
BS = 256
PB = 3
KB = 16
OWNER_SLOT_COUNT = 2
NB = 64
CHILD_ORDER_SIZE = 4096
TOTAL_SLOTS = 8
N_ROW = 4
N_COL = 8


def draw_owner_slots(key, part):
    key_count = jax.random.fold_in(key, 21)
    key_full = jax.random.fold_in(key, 22)
    key_short = jax.random.fold_in(key, 23)
    counts = jax.random.randint(key_count, (N_ROW,), 1, OWNER_SLOT_COUNT + 1)
    full_owner = jax.random.randint(key_full, (), 0, N_ROW)
    short_owner = (full_owner + 1) % N_ROW
    short_count = jax.random.randint(key_short, (), 1, OWNER_SLOT_COUNT)
    owner_ids = jnp.arange(N_ROW)
    counts = jnp.where(owner_ids == short_owner, short_count, counts)
    counts = jnp.where(owner_ids == full_owner, OWNER_SLOT_COUNT, counts)
    slot_position = jnp.arange(TOTAL_SLOTS) % OWNER_SLOT_COUNT
    owner_position = jnp.arange(TOTAL_SLOTS) // OWNER_SLOT_COUNT
    return (slot_position < counts[owner_position]).astype(jnp.int32)


def draw_child_rows(key, part):
    offset_key = jax.random.fold_in(key, 31)
    selection_key = jax.random.fold_in(key, 32)
    group_size = KB // N_COL
    cycle_total = NB // N_COL
    slot_offsets = jax.random.permutation(offset_key, TOTAL_SLOTS) % N_COL
    position = jnp.arange(KB)
    residue = (position[None, :] // group_size + slot_offsets[:, None]) % N_COL
    random_scores = jax.random.randint(selection_key, (TOTAL_SLOTS, N_COL, cycle_total), 0, 1 << 20)
    pick_order = jnp.argsort(random_scores * cycle_total + jnp.arange(cycle_total), axis=2)
    slot_position = jnp.arange(TOTAL_SLOTS)[:, None]
    cycle_pick = pick_order[slot_position, residue, position[None, :] % group_size]
    return (residue + N_COL * cycle_pick).astype(jnp.int32)


def with_ends(result, key, least, largest):
    index_at = [jax.random.randint(jax.random.fold_in(key, axis), (), 0, length) for axis, length in enumerate(result.shape)]
    widest = result.shape.index(max(result.shape))
    neighbour = index_at[:widest] + [(index_at[widest] + 1) % result.shape[widest]] + index_at[widest + 1:]
    return result.at[tuple(index_at)].set(least).at[tuple(neighbour)].set(largest)


def levels(own_key, extent, pieces, low, top_value):
    loudness, own = 1.0, jax.random.fold_in(own_key, 6)
    for dim, shards_of in pieces:
        draws = jnp.exp(jax.random.uniform(jax.random.fold_in(own, dim), (shards_of,), jnp.float32, low / len(pieces), top_value / len(pieces)))
        loudness = loudness * jnp.repeat(draws, extent[dim] // shards_of).reshape([-1 if axis == dim else 1 for axis in range(len(extent))])
    return loudness


def gaussian(own_key, shape, width, most, cuts=(), kind=jnp.bfloat16):
    entries = jax.random.normal(own_key, shape, jnp.float32) * width
    if len(cuts) > 0:
        entries = levels(own_key, shape, cuts, -0.22, 0.18) * entries
    return jnp.clip(entries, min=-most, max=most).astype(kind)


def setup_inputs(seed: int = 0) -> dict:
    seeds = jax.random.split(jax.random.key(seed), 7)
    front = gaussian(seeds[0], (NB // N_ROW, N_ROW * BS, NB // N_COL, N_COL * BS), 1.0, 6.0, ((1, 4), (3, 8)), jnp.float32)
    children = gaussian(seeds[1], (TOTAL_SLOTS, CHILD_ORDER_SIZE, CHILD_ORDER_SIZE), 1.0, 6.0, ((0, 4), (2, 8)), jnp.float32)
    child_rows = draw_child_rows(jax.random.fold_in(seeds[6], 71), 0)
    owner_slots = draw_owner_slots(jax.random.fold_in(seeds[6], 71), 0)
    inverses = gaussian(seeds[4], (PB, BS, BS), (BS * (4 * PB + BS // 4)) ** -0.5, 0.0390625, (), jnp.float32)
    pattern = with_ends((jax.random.randint(seeds[5], (NB, NB), 0, 4) < 3).astype(jnp.int32), jax.random.fold_in(seeds[5], 1), 0, 1)
    return {"front": front, "children": children, "child_rows": child_rows, "owner_slots": owner_slots, "inverses": inverses, "pattern": pattern}


precise = lax.Precision.HIGHEST


def reference(front, children, child_rows, owner_slots, inverses, pattern):
    front_block_list = front.reshape(NB, BS, NB, BS)

    def scatter_child_block(slot_index, running):
        child_block = lax.dynamic_index_in_dim(children, slot_index, 0, keepdims=False).reshape(KB, BS, KB, BS)
        child_block = jnp.transpose(child_block, (0, 2, 1, 3))
        child_block = child_block * lax.dynamic_index_in_dim(owner_slots, slot_index, 0, keepdims=False).astype(running.dtype)
        row_list = lax.dynamic_index_in_dim(child_rows, slot_index, 0, keepdims=False)
        return running.at[row_list[:, None], :, row_list[None, :], :].add(child_block)

    summed_front = lax.fori_loop(0, TOTAL_SLOTS, scatter_child_block, front_block_list)
    front_full = summed_front.reshape(F, F)
    block_of_row = jnp.arange(F, dtype=jnp.int32) // BS
    factors = []
    for step_index in range(PB):
        column = front_full[:, step_index * BS:(step_index + 1) * BS]
        for earlier in range(step_index):
            earlier_factor = factors[earlier]
            column = column - jnp.dot(earlier_factor, earlier_factor[step_index * BS:(step_index + 1) * BS].T, precision=precise)
        factor = jnp.dot(column, inverses[step_index].T, precision=precise)
        factor = jnp.where((block_of_row >= step_index)[:, None], factor, jnp.zeros_like(factor))
        factors.append(factor)
    lower = jnp.concatenate(factors, axis=1)
    tail_rows = lower[PB * BS:]
    update = jnp.dot(tail_rows, tail_rows.T, precision=precise)
    block_mask = pattern[PB:, PB:] > 0
    update_mask = jnp.repeat(jnp.repeat(block_mask, BS, axis=0), BS, axis=1)
    corner = front_full[PB * BS:, PB * BS:]
    corner = jnp.where(update_mask, corner - update, corner)
    result_full = front_full.at[PB * BS:, PB * BS:].set(corner)
    result_full = result_full.at[:, :PB * BS].set(lower)
    return result_full.reshape(NB // N_ROW, N_ROW * BS, NB // N_COL, N_COL * BS)
```

```python
import functools

import jax
import jax.numpy as jnp
from jax import lax
from jax.experimental import pallas as pl
from jax.experimental.pallas import tpu as pltpu
from jax.sharding import PartitionSpec as P

DEPTH = 4


def copy_kernel(order_ref, cols_ref, in_ref, out_ref):
    out_ref[...] = in_ref[...].reshape(out_ref.shape)


def pack_rows(blocks, order, cols, rows_n, tile):
    slots, kblocks, _, _ = blocks.shape
    per_row = kblocks // rows_n
    spec = pltpu.PrefetchScalarGridSpec(
        num_scalar_prefetch=2,
        grid=(rows_n, slots, per_row),
        in_specs=[pl.BlockSpec((1, 1, tile, tile), lambda r, s, p, o, c: (s, o[s * kblocks + r * per_row + p], 0, c[s]))],
        out_specs=pl.BlockSpec((1, 1, 1, tile, tile), lambda r, s, p, o, c: (r, s, p, 0, 0)),
    )
    return pl.pallas_call(
        copy_kernel,
        grid_spec=spec,
        out_shape=jax.ShapeDtypeStruct((rows_n, slots, per_row, tile, tile), blocks.dtype),
        name="pack_rows",
    )(order.reshape(-1), cols, blocks)


def pack_slots(blocks, order):
    shape = blocks.shape
    spec = pltpu.PrefetchScalarGridSpec(
        num_scalar_prefetch=2,
        grid=(shape[0],),
        in_specs=[pl.BlockSpec((1,) + shape[1:], lambda i, o, c: (o[i], 0, 0, 0))],
        out_specs=pl.BlockSpec((1,) + shape[1:], lambda i, o, c: (i, 0, 0, 0)),
    )
    return pl.pallas_call(
        copy_kernel,
        grid_spec=spec,
        out_shape=jax.ShapeDtypeStruct(shape, blocks.dtype),
        compiler_params=pltpu.CompilerParams(vmem_limit_bytes=24 << 20),
        name="pack_slots",
    )(order, order, blocks)


def event_copies(index, pieces, buf, sems, event_ref):
    lane = lax.rem(index, DEPTH)
    return [
        pltpu.make_async_copy(piece.at[event_ref[index]], buf.at[lane, t], sems.at[lane, t])
        for t, piece in enumerate(pieces)
    ]


def run_events(a, start_ref, event_ref, steps, pieces, buf, sems, add):
    total = start_ref[steps]

    @pl.when(a == 0)
    def _():
        for first in range(DEPTH):
            @pl.when(first < total)
            def _():
                for copy in event_copies(jnp.int32(first), pieces, buf, sems, event_ref):
                    copy.start()

    def body(index, carry):
        for copy in event_copies(index, pieces, buf, sems, event_ref):
            copy.wait()
        add(index, lax.rem(index, DEPTH))

        @pl.when(index + DEPTH < total)
        def _():
            for copy in event_copies(index + DEPTH, pieces, buf, sems, event_ref):
                copy.start()

        return carry

    lax.fori_loop(start_ref[a], start_ref[a + 1], body, 0)


def panel_kernel(steps, start_ref, event_ref, front_ref, piece_ref, out_ref, buf, sems):
    a = pl.program_id(0)
    out_ref[...] = front_ref[...]

    def add(index, lane):
        out_ref[0] = out_ref[0] + buf[lane, 0]

    run_events(a, start_ref, event_ref, steps, [piece_ref], buf, sems, add)


def panel_sum(first, start, events, piece):
    steps, tile, _ = first.shape
    spec = pltpu.PrefetchScalarGridSpec(
        num_scalar_prefetch=2,
        grid=(steps,),
        in_specs=[pl.BlockSpec((1, tile, tile), lambda a, s, e: (a, 0, 0)), pl.BlockSpec(memory_space=pl.ANY)],
        out_specs=pl.BlockSpec((1, tile, tile), lambda a, s, e: (a, 0, 0)),
        scratch_shapes=[pltpu.VMEM((DEPTH, 1, tile, tile), jnp.float32), pltpu.SemaphoreType.DMA((DEPTH, 1))],
    )
    return pl.pallas_call(
        functools.partial(panel_kernel, steps),
        grid_spec=spec,
        out_shape=jax.ShapeDtypeStruct(first.shape, jnp.float32),
        name="panel_sum",
    )(start, events, first, piece)


def halves(x):
    high = x.astype(jnp.bfloat16)
    return high, (x - high.astype(jnp.float32)).astype(jnp.bfloat16)


def dot3(left, right):
    def one(u, v):
        return lax.dot_general(u, v, (((1,), (1,)), ((), ())), preferred_element_type=jnp.float32)

    return one(left[0], right[0]) + (one(left[0], right[1]) + one(left[1], right[0]))


def final_kernel(sizes, place_ref, mask_ref, start_ref, event_ref, target_ref, *refs):
    steps, cols, tile, panel, rows_n, cols_n, parts = sizes
    front_ref, panel_ref, across_ref, top_ref, inv_ref = refs[:5]
    pieces = list(refs[5:5 + parts])
    out_ref, wide_hi, wide_lo, top_hi, top_lo, inv_hi, inv_lo, buf, sems = refs[5 + parts:]
    a = pl.program_id(0)
    my_row, my_col = place_ref[0], place_ref[1]

    def cut(j):
        return slice(j * tile, (j + 1) * tile)

    def factor(load, count, block):
        got = []
        for j in range(count):
            column = load(j)
            for i in range(j):
                column = column - dot3(got[i][1], (top_hi[j, i], top_lo[j, i]))
            value = dot3(halves(column), (inv_hi[j], inv_lo[j]))
            value = jnp.where(block >= j, value, jnp.zeros_like(value))
            got.append((value, halves(value)))
        return got

    @pl.when(a == 0)
    def _():
        for j in range(panel):
            inv_hi[j], inv_lo[j] = halves(inv_ref[j])
        for row in range(1, panel):
            for i, (_, pair) in enumerate(factor(lambda j: top_ref[row, :, cut(j)], row, row)):
                top_hi[row, i], top_lo[row, i] = pair

        def widen(b, carry):
            for j, (_, pair) in enumerate(factor(lambda j: across_ref[b, :, cut(j)], panel, b * cols_n + my_col)):
                wide_hi[b, :, cut(j)], wide_lo[b, :, cut(j)] = pair
            return carry

        lax.fori_loop(0, cols, widen, 0)

    mine = factor(lambda j: panel_ref[0, :, cut(j)], panel, a * rows_n + my_row)
    high = jnp.concatenate([pair[0] for _, pair in mine], axis=1)
    low = jnp.concatenate([pair[1] for _, pair in mine], axis=1)
    for b in range(cols):
        update = dot3((high, low), (wide_hi[b], wide_lo[b]))
        for h in range(0, tile, 128):
            block = front_ref[0, :, b, h:h + 128]
            out_ref[0, :, b, h:h + 128] = jnp.where(mask_ref[a * cols + b] > 0, block - update[:, h:h + 128], block)

    def add(index, lane):
        for t in range(parts):
            for b in range(cols):
                @pl.when(target_ref[index * parts + t] == b)
                def _():
                    out_ref[0, :, b, :] = out_ref[0, :, b, :] + buf[lane, t]

    run_events(a, start_ref, event_ref, steps, pieces, buf, sems, add)
    for j in range(panel):
        @pl.when(my_col == j)
        def _():
            out_ref[0, :, 0, :] = mine[j][0]


def final_step(front, panel_s, across_s, top_s, inverses, pieces, place, mask, start, events, targets, rows_n, cols_n):
    steps, tile, cols, _ = front.shape
    panel = inverses.shape[0]
    parts = len(pieces)
    whole = pl.BlockSpec(memory_space=pltpu.VMEM)
    spec = pltpu.PrefetchScalarGridSpec(
        num_scalar_prefetch=5,
        grid=(steps,),
        in_specs=[
            pl.BlockSpec((1, tile, cols, tile), lambda a, *_: (a, 0, 0, 0)),
            pl.BlockSpec((1, tile, panel * tile), lambda a, *_: (a, 0, 0)),
            whole,
            whole,
            whole,
        ] + [pl.BlockSpec(memory_space=pl.ANY)] * parts,
        out_specs=pl.BlockSpec((1, tile, cols, tile), lambda a, *_: (a, 0, 0, 0)),
        scratch_shapes=[
            pltpu.VMEM((cols, tile, panel * tile), jnp.bfloat16),
            pltpu.VMEM((cols, tile, panel * tile), jnp.bfloat16),
            pltpu.VMEM((panel, panel, tile, tile), jnp.bfloat16),
            pltpu.VMEM((panel, panel, tile, tile), jnp.bfloat16),
            pltpu.VMEM((panel, tile, tile), jnp.bfloat16),
            pltpu.VMEM((panel, tile, tile), jnp.bfloat16),
            pltpu.VMEM((DEPTH, parts, tile, tile), jnp.float32),
            pltpu.SemaphoreType.DMA((DEPTH, parts)),
        ],
    )
    sizes = (steps, cols, tile, panel, rows_n, cols_n, parts)
    return pl.pallas_call(
        functools.partial(final_kernel, sizes),
        grid_spec=spec,
        out_shape=jax.ShapeDtypeStruct(front.shape, jnp.float32),
        compiler_params=pltpu.CompilerParams(vmem_limit_bytes=52 << 20),
        cost_estimate=pl.CostEstimate(
            flops=6 * front.size * panel * tile, bytes_accessed=10 * front.size, transcendentals=0
        ),
        name="final_step",
    )(place, mask, start, events, targets, front, panel_s, across_s, top_s, inverses, *pieces)


def event_list(keys, steps):
    order = jnp.argsort(keys).astype(jnp.int32)
    start = jnp.sum(keys[None, :] < jnp.arange(steps + 1)[:, None], axis=1).astype(jnp.int32)
    return order, start


def shards(front, children, child_rows, owner_slots, inverses, pattern):
    rows_n = lax.axis_size("row")
    cols_n = lax.axis_size("col")
    my_row = lax.axis_index("row")
    my_col = lax.axis_index("col")
    local_rows, tile, local_cols, _ = front.shape
    slots_here, child_order, child_width = children.shape
    kblocks = child_order // tile
    per_row = kblocks // rows_n
    per_col = child_width // tile
    slot_total = child_rows.shape[0]
    per_dest = slot_total // cols_n
    panel = inverses.shape[0]

    position = jnp.arange(kblocks, dtype=jnp.int32)
    row_order = jnp.argsort(child_rows % rows_n * kblocks + position[None, :], axis=1).astype(jnp.int32)
    my_order = lax.dynamic_slice_in_dim(row_order, my_row * slots_here, slots_here, 0)
    my_rank = lax.dynamic_slice_in_dim(row_order, my_row * per_row, per_row, 1)
    row_blocks = jnp.take_along_axis(child_rows, my_rank, axis=1)
    col_blocks = child_rows.reshape(slot_total, cols_n, per_col)
    col_pick = jnp.argsort(col_blocks, axis=2).astype(jnp.int32)
    col_sorted = jnp.sort(col_blocks, axis=2)
    my_pick = lax.dynamic_slice(col_pick, (my_row * slots_here, my_col, 0), (slots_here, 1, per_col))[:, 0]
    slot_ids = jnp.arange(slot_total, dtype=jnp.int32)
    dest_by_src = jnp.transpose(col_blocks[:, :, 0] % cols_n)
    send_order = jnp.argsort(dest_by_src * slot_total + slot_ids[None, :], axis=1).astype(jnp.int32)
    my_send = lax.dynamic_index_in_dim(send_order, my_col, 0, keepdims=False)

    blocks_in = children.reshape(slots_here, kblocks, tile, child_width)
    pieces = []
    for t in range(per_col):
        outgoing = pack_rows(blocks_in, my_order, my_pick[:, t], rows_n, tile)
        arrived = lax.all_to_all(outgoing, "row", split_axis=0, concat_axis=0, tiled=True)
        arrived = arrived.reshape(slot_total, per_row, tile, tile)
        outgoing = pack_slots(arrived, my_send)
        landed = lax.all_to_all(outgoing, "col", split_axis=0, concat_axis=0, tiled=True)
        pieces.append(landed.reshape(slot_total * per_row, tile, tile))

    recv_slot = lax.dynamic_slice_in_dim(send_order, my_col * per_dest, per_dest, 1)
    src_ids = jnp.arange(cols_n, dtype=jnp.int32)
    got_rows = row_blocks[recv_slot] // rows_n
    got_cols = (col_sorted[recv_slot, src_ids[:, None]] // cols_n).astype(jnp.int32)
    live = (owner_slots[recv_slot] > 0)[:, :, None]
    keys = jnp.where(live, got_rows, local_rows).reshape(-1)
    panel_keys = jnp.where(live & (got_cols[:, :, :1] == 0), got_rows, local_rows).reshape(-1)
    events, start = event_list(keys, local_rows)
    panel_events, panel_start = event_list(panel_keys, local_rows)
    targets = got_cols.reshape(cols_n * per_dest, per_col)[events // per_row].reshape(-1)

    current = panel_sum(front[:, :, 0, :], panel_start, panel_events, pieces[0])
    spread = jnp.concatenate(
        [jnp.where(my_col == j, current, jnp.zeros_like(current)) for j in range(panel)], axis=2
    )
    panel_s = lax.psum(spread, "col")

    ratio = cols_n // rows_n
    split = panel_s.reshape(local_cols, ratio, tile, panel * tile)
    chosen = lax.dynamic_index_in_dim(split, my_col // rows_n, 1, keepdims=False)
    tops = jnp.stack(
        [jnp.where(my_row == i % rows_n, panel_s[i // rows_n], jnp.zeros_like(panel_s[0])) for i in range(panel)]
    )
    chosen = jnp.where(my_row == my_col % rows_n, chosen, jnp.zeros_like(chosen))
    across_s, top_s = lax.psum((chosen, tops), "row")

    row_ids = jnp.arange(local_rows, dtype=jnp.int32) * rows_n + my_row
    col_ids = jnp.arange(local_cols, dtype=jnp.int32) * cols_n + my_col
    mask = pattern.reshape(local_rows, rows_n, local_cols, cols_n)
    mask = lax.dynamic_index_in_dim(mask, my_row, 1, keepdims=False)
    mask = lax.dynamic_index_in_dim(mask, my_col, 2, keepdims=False)
    mask = (mask > 0) & (row_ids >= panel)[:, None] & (col_ids >= panel)[None, :]
    place = jnp.stack([my_row, my_col]).astype(jnp.int32)
    return final_step(
        front, panel_s, across_s, top_s, inverses, pieces, place,
        mask.astype(jnp.int32).reshape(-1), start, events, targets, rows_n, cols_n,
    )


def solution(mesh):
    return jax.shard_map(
        shards,
        mesh=mesh,
        in_specs=(P(None, "row", None, "col"), P("row", None, "col"), P(), P(), P(), P()),
        out_specs=P(None, "row", None, "col"),
        check_vma=False,
    )
```

```python
import functools

import jax
import jax.numpy as jnp
from jax import lax
from jax.experimental import pallas as pl
from jax.experimental.pallas import tpu as pltpu
from jax.sharding import PartitionSpec as P

DEPTH = 4


def copy_kernel(order_ref, cols_ref, in_ref, out_ref):
    out_ref[...] = in_ref[...].reshape(out_ref.shape)


def pack_rows(blocks, order, cols, rows_n, tile):
    slots, kblocks, _, _ = blocks.shape
    per_row = kblocks // rows_n
    spec = pltpu.PrefetchScalarGridSpec(
        num_scalar_prefetch=2,
        grid=(rows_n, slots, per_row),
        in_specs=[pl.BlockSpec((1, 1, tile, tile), lambda r, s, p, o, c: (s, o[s * kblocks + r * per_row + p], 0, c[s]))],
        out_specs=pl.BlockSpec((1, 1, 1, tile, tile), lambda r, s, p, o, c: (r, s, p, 0, 0)),
    )
    return pl.pallas_call(
        copy_kernel,
        grid_spec=spec,
        out_shape=jax.ShapeDtypeStruct((rows_n, slots, per_row, tile, tile), blocks.dtype),
        name="pack_rows",
    )(order.reshape(-1), cols, blocks)


def pack_slots(blocks, order):
    shape = blocks.shape
    spec = pltpu.PrefetchScalarGridSpec(
        num_scalar_prefetch=2,
        grid=(shape[0],),
        in_specs=[pl.BlockSpec((1,) + shape[1:], lambda i, o, c: (o[i], 0, 0, 0))],
        out_specs=pl.BlockSpec((1,) + shape[1:], lambda i, o, c: (i, 0, 0, 0)),
    )
    return pl.pallas_call(
        copy_kernel,
        grid_spec=spec,
        out_shape=jax.ShapeDtypeStruct(shape, blocks.dtype),
        compiler_params=pltpu.CompilerParams(vmem_limit_bytes=24 << 20),
        name="pack_slots",
    )(order, order, blocks)


def event_copies(index, pieces, buf, sems, event_ref):
    lane = lax.rem(index, DEPTH)
    return [
        pltpu.make_async_copy(piece.at[event_ref[index]], buf.at[lane, t], sems.at[lane, t])
        for t, piece in enumerate(pieces)
    ]


def run_events(a, start_ref, event_ref, steps, pieces, buf, sems, add):
    total = start_ref[steps]

    @pl.when(a == 0)
    def _():
        for first in range(DEPTH):
            @pl.when(first < total)
            def _():
                for copy in event_copies(jnp.int32(first), pieces, buf, sems, event_ref):
                    copy.start()

    def body(index, carry):
        for copy in event_copies(index, pieces, buf, sems, event_ref):
            copy.wait()
        add(index, lax.rem(index, DEPTH))

        @pl.when(index + DEPTH < total)
        def _():
            for copy in event_copies(index + DEPTH, pieces, buf, sems, event_ref):
                copy.start()

        return carry

    lax.fori_loop(start_ref[a], start_ref[a + 1], body, 0)


def panel_kernel(steps, start_ref, event_ref, front_ref, piece_ref, out_ref, buf, sems):
    a = pl.program_id(0)
    out_ref[...] = front_ref[...]

    def add(index, lane):
        out_ref[0] = out_ref[0] + buf[lane, 0]

    run_events(a, start_ref, event_ref, steps, [piece_ref], buf, sems, add)


def panel_sum(first, start, events, piece):
    steps, tile, _ = first.shape
    spec = pltpu.PrefetchScalarGridSpec(
        num_scalar_prefetch=2,
        grid=(steps,),
        in_specs=[pl.BlockSpec((1, tile, tile), lambda a, s, e: (a, 0, 0)), pl.BlockSpec(memory_space=pl.ANY)],
        out_specs=pl.BlockSpec((1, tile, tile), lambda a, s, e: (a, 0, 0)),
        scratch_shapes=[pltpu.VMEM((DEPTH, 1, tile, tile), jnp.float32), pltpu.SemaphoreType.DMA((DEPTH, 1))],
    )
    return pl.pallas_call(
        functools.partial(panel_kernel, steps),
        grid_spec=spec,
        out_shape=jax.ShapeDtypeStruct(first.shape, jnp.float32),
        name="panel_sum",
    )(start, events, first, piece)


def halves(x):
    high = x.astype(jnp.bfloat16)
    return high, (x - high.astype(jnp.float32)).astype(jnp.bfloat16)


def dot3(left, right):
    def one(u, v):
        return lax.dot_general(u, v, (((1,), (1,)), ((), ())), preferred_element_type=jnp.float32)

    return one(left[0], right[0]) + (one(left[0], right[1]) + one(left[1], right[0]))


def final_kernel(sizes, place_ref, mask_ref, start_ref, event_ref, target_ref, *refs):
    steps, cols, tile, panel, rows_n, cols_n, parts = sizes
    front_ref, top_ref, inv_ref = refs[:3]
    panel_refs = refs[3:3 + panel]
    across_refs = refs[3 + panel:3 + 2 * panel]
    pieces = list(refs[3 + 2 * panel:3 + 2 * panel + parts])
    out_ref, wide_hi, wide_lo, top_hi, top_lo, inv_hi, inv_lo, buf, sems = refs[3 + 2 * panel + parts:]
    a = pl.program_id(0)
    my_row, my_col = place_ref[0], place_ref[1]

    def cut(j):
        return slice(j * tile, (j + 1) * tile)

    def factor(load, count, block):
        got = []
        for j in range(count):
            column = load(j)
            for i in range(j):
                column = column - dot3(got[i][1], (top_hi[j, i], top_lo[j, i]))
            value = dot3(halves(column), (inv_hi[j], inv_lo[j]))
            value = jnp.where(block >= j, value, jnp.zeros_like(value))
            got.append((value, halves(value)))
        return got

    @pl.when(a == 0)
    def _():
        for j in range(panel):
            inv_hi[j], inv_lo[j] = halves(inv_ref[j])
        for row in range(1, panel):
            for i, (_, pair) in enumerate(factor(lambda j: top_ref[row, :, cut(j)], row, row)):
                top_hi[row, i], top_lo[row, i] = pair

        def widen(b, carry):
            for j, (_, pair) in enumerate(factor(lambda j: across_refs[j][b], panel, b * cols_n + my_col)):
                wide_hi[b, :, cut(j)], wide_lo[b, :, cut(j)] = pair
            return carry

        lax.fori_loop(0, cols, widen, 0)

    mine = factor(lambda j: panel_refs[j][0], panel, a * rows_n + my_row)
    high = jnp.concatenate([pair[0] for _, pair in mine], axis=1)
    low = jnp.concatenate([pair[1] for _, pair in mine], axis=1)
    for b in range(cols):
        update = dot3((high, low), (wide_hi[b], wide_lo[b]))
        for h in range(0, tile, 128):
            block = front_ref[0, :, b, h:h + 128]
            out_ref[0, :, b, h:h + 128] = jnp.where(mask_ref[a * cols + b] > 0, block - update[:, h:h + 128], block)

    def add(index, lane):
        for t in range(parts):
            for b in range(cols):
                @pl.when(target_ref[index * parts + t] == b)
                def _():
                    out_ref[0, :, b, :] = out_ref[0, :, b, :] + buf[lane, t]

    run_events(a, start_ref, event_ref, steps, pieces, buf, sems, add)
    for j in range(panel):
        @pl.when(my_col == j)
        def _():
            out_ref[0, :, 0, :] = mine[j][0]


def final_step(front, panel_s, across_s, top_s, inverses, pieces, place, mask, start, events, targets, rows_n, cols_n):
    steps, tile, cols, _ = front.shape
    panel = inverses.shape[0]
    parts = len(pieces)
    whole = pl.BlockSpec(memory_space=pltpu.VMEM)
    spec = pltpu.PrefetchScalarGridSpec(
        num_scalar_prefetch=5,
        grid=(steps,),
        in_specs=[
            pl.BlockSpec((1, tile, cols, tile), lambda a, *_: (a, 0, 0, 0)),
            whole,
            whole,
        ] + [pl.BlockSpec((1, tile, tile), lambda a, *_: (a, 0, 0))] * panel + [whole] * panel + [pl.BlockSpec(memory_space=pl.ANY)] * parts,
        out_specs=pl.BlockSpec((1, tile, cols, tile), lambda a, *_: (a, 0, 0, 0)),
        scratch_shapes=[
            pltpu.VMEM((cols, tile, panel * tile), jnp.bfloat16),
            pltpu.VMEM((cols, tile, panel * tile), jnp.bfloat16),
            pltpu.VMEM((panel, panel, tile, tile), jnp.bfloat16),
            pltpu.VMEM((panel, panel, tile, tile), jnp.bfloat16),
            pltpu.VMEM((panel, tile, tile), jnp.bfloat16),
            pltpu.VMEM((panel, tile, tile), jnp.bfloat16),
            pltpu.VMEM((DEPTH, parts, tile, tile), jnp.float32),
            pltpu.SemaphoreType.DMA((DEPTH, parts)),
        ],
    )
    sizes = (steps, cols, tile, panel, rows_n, cols_n, parts)
    return pl.pallas_call(
        functools.partial(final_kernel, sizes),
        grid_spec=spec,
        out_shape=jax.ShapeDtypeStruct(front.shape, jnp.float32),
        compiler_params=pltpu.CompilerParams(vmem_limit_bytes=52 << 20),
        cost_estimate=pl.CostEstimate(
            flops=6 * front.size * panel * tile, bytes_accessed=10 * front.size, transcendentals=0
        ),
        name="final_step",
    )(place, mask, start, events, targets, front, top_s, inverses, *panel_s, *across_s, *pieces)


def event_list(keys, steps):
    order = jnp.argsort(keys).astype(jnp.int32)
    start = jnp.sum(keys[None, :] < jnp.arange(steps + 1)[:, None], axis=1).astype(jnp.int32)
    return order, start


def row_spread(block, rows_n, cols_n, my_row, my_col):
    half = block.shape[0] // 2
    steps = [1 << k for k in range((rows_n - 1).bit_length())]
    apart = my_row ^ (my_col % rows_n)
    done = []
    for part, order in ((block[:half], steps), (block[half:], steps[::-1])):
        held = [0]
        for step in order:
            pairs = [
                (((c % rows_n) ^ h) * cols_n + c, ((c % rows_n) ^ h ^ step) * cols_n + c)
                for c in range(cols_n) for h in held
            ]
            came = lax.ppermute(part, ("row", "col"), pairs)
            fresh = functools.reduce(jnp.logical_or, [apart == (h ^ step) for h in held])
            part = jnp.where(fresh, came, part)
            held = held + [h ^ step for h in held]
        done.append(part)
    return jnp.concatenate(done, axis=0)


def shards(front, children, child_rows, owner_slots, inverses, pattern):
    rows_n = lax.axis_size("row")
    cols_n = lax.axis_size("col")
    my_row = lax.axis_index("row")
    my_col = lax.axis_index("col")
    local_rows, tile, local_cols, _ = front.shape
    slots_here, child_order, child_width = children.shape
    kblocks = child_order // tile
    per_row = kblocks // rows_n
    per_col = child_width // tile
    slot_total = child_rows.shape[0]
    per_dest = slot_total // cols_n
    panel = inverses.shape[0]

    position = jnp.arange(kblocks, dtype=jnp.int32)
    row_order = jnp.argsort(child_rows % rows_n * kblocks + position[None, :], axis=1).astype(jnp.int32)
    my_order = lax.dynamic_slice_in_dim(row_order, my_row * slots_here, slots_here, 0)
    my_rank = lax.dynamic_slice_in_dim(row_order, my_row * per_row, per_row, 1)
    row_blocks = jnp.take_along_axis(child_rows, my_rank, axis=1)
    col_blocks = child_rows.reshape(slot_total, cols_n, per_col)
    col_pick = jnp.argsort(col_blocks, axis=2).astype(jnp.int32)
    col_sorted = jnp.sort(col_blocks, axis=2)
    my_pick = lax.dynamic_slice(col_pick, (my_row * slots_here, my_col, 0), (slots_here, 1, per_col))[:, 0]
    slot_ids = jnp.arange(slot_total, dtype=jnp.int32)
    dest_by_src = jnp.transpose(col_blocks[:, :, 0] % cols_n)
    send_order = jnp.argsort(dest_by_src * slot_total + slot_ids[None, :], axis=1).astype(jnp.int32)
    my_send = lax.dynamic_index_in_dim(send_order, my_col, 0, keepdims=False)

    blocks_in = children.reshape(slots_here, kblocks, tile, child_width)
    pieces = []
    for t in range(per_col):
        outgoing = pack_rows(blocks_in, my_order, my_pick[:, t], rows_n, tile)
        arrived = lax.all_to_all(outgoing, "row", split_axis=0, concat_axis=0, tiled=True)
        arrived = arrived.reshape(slot_total, per_row, tile, tile)
        outgoing = pack_slots(arrived, my_send)
        landed = lax.all_to_all(outgoing, "col", split_axis=0, concat_axis=0, tiled=True)
        pieces.append(landed.reshape(slot_total * per_row, tile, tile))

    recv_slot = lax.dynamic_slice_in_dim(send_order, my_col * per_dest, per_dest, 1)
    src_ids = jnp.arange(cols_n, dtype=jnp.int32)
    got_rows = row_blocks[recv_slot] // rows_n
    got_cols = (col_sorted[recv_slot, src_ids[:, None]] // cols_n).astype(jnp.int32)
    live = (owner_slots[recv_slot] > 0)[:, :, None]
    keys = jnp.where(live, got_rows, local_rows).reshape(-1)
    panel_keys = jnp.where(live & (got_cols[:, :, :1] == 0), got_rows, local_rows).reshape(-1)
    events, start = event_list(keys, local_rows)
    panel_events, panel_start = event_list(panel_keys, local_rows)
    targets = got_cols.reshape(cols_n * per_dest, per_col)[events // per_row].reshape(-1)

    current = panel_sum(front[:, :, 0, :], panel_start, panel_events, pieces[0])
    ratio = cols_n // rows_n
    panel_s, across_s = [], []
    for j in range(panel):
        column = lax.psum(jnp.where(my_col == j, current, jnp.zeros_like(current)), "col")
        current, column = lax.optimization_barrier((current, column))
        split = column.reshape(local_cols, ratio, tile, tile)
        chosen = lax.dynamic_index_in_dim(split, my_col // rows_n, 1, keepdims=False)
        panel_s.append(column)
        across_s.append(row_spread(chosen, rows_n, cols_n, my_row, my_col))
    tops = jnp.stack([
        jnp.concatenate([
            jnp.where(my_row == i % rows_n, panel_s[j][i // rows_n], jnp.zeros_like(panel_s[0][0]))
            for j in range(panel - 1)
        ], axis=1)
        for i in range(panel)
    ])
    top_s = lax.psum(tops, "row")

    row_ids = jnp.arange(local_rows, dtype=jnp.int32) * rows_n + my_row
    col_ids = jnp.arange(local_cols, dtype=jnp.int32) * cols_n + my_col
    mask = pattern.reshape(local_rows, rows_n, local_cols, cols_n)
    mask = lax.dynamic_index_in_dim(mask, my_row, 1, keepdims=False)
    mask = lax.dynamic_index_in_dim(mask, my_col, 2, keepdims=False)
    mask = (mask > 0) & (row_ids >= panel)[:, None] & (col_ids >= panel)[None, :]
    place = jnp.stack([my_row, my_col]).astype(jnp.int32)
    return final_step(
        front, panel_s, across_s, top_s, inverses, pieces, place,
        mask.astype(jnp.int32).reshape(-1), start, events, targets, rows_n, cols_n,
    )


def solution(mesh):
    return jax.shard_map(
        shards,
        mesh=mesh,
        in_specs=(P(None, "row", None, "col"), P("row", None, "col"), P(), P(), P(), P()),
        out_specs=P(None, "row", None, "col"),
        check_vma=False,
    )
```
